1024 devices in a mesh: dom: 16 (over x, core), grp: 64 (over y, z).
Axes of the slice: x: 8, y: 8, z: 8, core: 2. Of those that a mesh axis runs over, the one named last changes fastest.
Arguments:
- features: bfloat16 [524288, 128], P(('dom', 'grp')), may hold values from -6 to 6
- hub_features: bfloat16 [32768, 128], P(('dom', 'grp')), may hold values from -6 to 6
- nbr_ids: int32 [524288, 12], P(('dom', 'grp')), may hold values from 0 to 1535, as said below
- hub_ids: int32 [524288, 4], P(('dom', 'grp')), may hold values from 0 to 2047, as said below
- halo_rows: int32 [16384, 64], P(('dom', 'grp')), may hold values from -1 to 511, as said below
- w_self: bfloat16 [128, 256], replicated, may hold values from -0.5 to 0.5
- w_neigh: bfloat16 [128, 256], replicated, may hold values from -0.5 to 0.5
- grad_hidden: bfloat16 [524288, 256], P(('dom', 'grp')), may hold values from -6 to 6
Outputs:
- hidden: bfloat16 [524288, 256], P(('dom', 'grp'))
- grad_features: float32 [524288, 128], P(('dom', 'grp'))
- grad_hubs: float32 [32768, 128], P(('dom', 'grp'))
- grad_w_self: float32 [128, 256], replicated
- grad_w_neigh: float32 [128, 256], replicated
The draws below stay inside these ranges and needn't reach their ends.
Inputs may be any that keep to these rules, and one draw needn't show every extreme that they name: `nbr_ids`: entries below 512 name the partition's own vertex; an entry 512 + p * 64 + j names slot j from peer p of the dom group, and only filled slots are named. `halo_rows`: in each row the filled slots come first and name distinct vertices; at least a quarter of a row's slots are filled, and each partition fills all 64 slots of one row. `hub_ids`: among the 2048 entries of one partition, exactly 512 * 4 / 64 name hubs in each block of 32 consecutive hub indices.
All inputs are finite; a program needn't handle non-finite values.
Results may differ from the reference program's by a relative error of at most 0.017.
The reference program's roundings to bfloat16 on the way (of `source_table`, `aggregate`, `grad_pre` and `grad_agg`) count: a program that leaves them out, or rounds other values in their place, can miss the bound.
Values may be sent and summed in bfloat16 or wider, within the bound.
No kernel may reach another device: no remote copies, remote signals or barrier semaphores. Data moves between devices by JAX's collectives and lax.ppermute only.
A program may use at most 32 MiB of HBM per device.

```python
import jax
import jax.numpy as jnp
from jax import lax

F = 128
H = 256
K = 12
HK = 4
V_DEV = 512
HALO = 64
HUB_DEV = 32
HUBS = 2048
VERTS = 524288
HUB_ALL = 32768
N_DOM = 16
N_GRP = 64


def peer_counts(key):
    counts = jax.random.randint(key, (N_DOM, N_GRP, N_DOM), HALO // 4, HALO + 1, dtype=jnp.int32)
    source_dom = jnp.arange(N_DOM, dtype=jnp.int32)[:, None, None]
    target_dom = jnp.arange(N_DOM, dtype=jnp.int32)[None, None, :]
    full_peer = target_dom == (source_dom + 1) % N_DOM
    return jnp.where(full_peer, HALO, counts)


def draw_halo_rows(key, part):
    counts = peer_counts(key)
    key = jax.random.fold_in(key, 11)
    scores = jax.random.randint(key, (N_DOM * N_GRP * N_DOM, V_DEV), 0, 2 ** 19, dtype=jnp.int32)
    scores = scores * V_DEV + jnp.arange(V_DEV, dtype=jnp.int32)[None, :]
    order = jnp.argsort(scores, axis=1)[:, :HALO].astype(jnp.int32)
    slot_index = jnp.arange(HALO, dtype=jnp.int32)[None, :]
    return jnp.where(slot_index < counts.reshape(-1, 1), order, -1).astype(jnp.int32)


def draw_nbr_ids(key, part):
    counts = peer_counts(key)
    key = jax.random.fold_in(key, 23)
    key_peer, key_slot, key_local, key_pick = jax.random.split(key, 4)
    incoming = counts.transpose(2, 1, 0)
    shape_all = (N_DOM, N_GRP, V_DEV, K)
    peer = jax.random.randint(key_peer, shape_all, 0, N_DOM, dtype=jnp.int32)
    live_count = jnp.take_along_axis(incoming, peer.reshape(N_DOM, N_GRP, V_DEV * K), axis=2).reshape(shape_all)
    slot_pick = jax.random.randint(key_slot, shape_all, 0, 2 ** 16, dtype=jnp.int32) % live_count
    local_pick = jax.random.randint(key_local, shape_all, 0, V_DEV, dtype=jnp.int32)
    choose_local = jax.random.randint(key_pick, shape_all, 0, 2, dtype=jnp.int32) == 0
    halo_pick = V_DEV + peer * HALO + slot_pick
    return jnp.where(choose_local, local_pick, halo_pick).reshape(N_DOM * N_GRP * V_DEV, K).astype(jnp.int32)


def draw_hub_ids(key, part):
    key = jax.random.fold_in(key, 37)
    key_perm, key_local = jax.random.split(key, 2)
    entries = V_DEV * HK
    owners = jnp.arange(entries, dtype=jnp.int32) % N_GRP
    device_keys = jax.random.split(key_perm, N_DOM * N_GRP)
    placed = jax.vmap(lambda k: jax.random.permutation(k, owners))(device_keys)
    local_pick = jax.random.randint(key_local, (N_DOM * N_GRP, entries), 0, HUB_DEV, dtype=jnp.int32)
    return (placed * HUB_DEV + local_pick).reshape(N_DOM * N_GRP * V_DEV, HK).astype(jnp.int32)


def shard_levels(key, extent, cuts, smallest, largest):
    loudness = 1.0
    for axis_at, parts in cuts:
        draws = jax.random.uniform(jax.random.fold_in(jax.random.fold_in(key, 6), axis_at), (parts,), jnp.float32, smallest / len(cuts), largest / len(cuts))
        loudness = loudness * jnp.repeat(jnp.exp(draws), extent[axis_at] // parts).reshape((-1,) + (1,) * (len(extent) - 1 - axis_at))
    return loudness


def normal_values(stream_key, dims, spread, reach, cuts=(), kind=jnp.bfloat16):
    array = jax.random.normal(stream_key, dims, jnp.float32) * spread
    if len(cuts) > 0:
        array = shard_levels(stream_key, dims, cuts, -0.22, 0.18) * array
    return jnp.clip(array, min=-reach, max=reach).astype(kind)


def setup_inputs(seed: int = 0) -> dict:
    streams_of = jax.random.split(jax.random.key(seed), 9)
    return {
        "features": normal_values(streams_of[0], (VERTS, F), 1.0, 6.0, ((0, 1024),)),
        "hub_features": normal_values(streams_of[1], (HUB_ALL, F), 1.0, 6.0, ((0, 1024),)),
        "nbr_ids": draw_nbr_ids(jax.random.fold_in(streams_of[8], 71), 0),
        "hub_ids": draw_hub_ids(jax.random.fold_in(streams_of[8], 71), 0),
        "halo_rows": draw_halo_rows(jax.random.fold_in(streams_of[8], 71), 0),
        "w_self": normal_values(streams_of[5], (F, H), F ** -0.5, 0.5),
        "w_neigh": normal_values(streams_of[6], (F, H), F ** -0.5, 0.5),
        "grad_hidden": normal_values(streams_of[7], (VERTS, H), 1.0, 6.0, ((0, 1024),)),
    }


def partition_step(source_table, nbr_part, hub_table, hub_part, own_rows, cot_rows, w_self, w_neigh):
    mean_scale = 1.0 / (K + HK)
    gathered = jax.vmap(lambda tab, idx: tab[idx])(source_table, nbr_part).astype(jnp.float32).sum(axis=2)
    hub_sum = hub_table[hub_part].astype(jnp.float32).sum(axis=2)
    aggregate = ((gathered + hub_sum) * mean_scale).astype(jnp.bfloat16).reshape(-1, F)
    own_flat = own_rows.reshape(-1, F)
    cot_flat = cot_rows.reshape(-1, H)
    preact = jnp.dot(own_flat, w_self, preferred_element_type=jnp.float32) + jnp.dot(aggregate, w_neigh, preferred_element_type=jnp.float32)
    hidden = jnp.maximum(preact, 0.0).astype(jnp.bfloat16)
    grad_pre = jnp.where(preact > 0, cot_flat.astype(jnp.float32), 0.0).astype(jnp.bfloat16)
    part_self = jnp.dot(own_flat.T, grad_pre, preferred_element_type=jnp.float32)
    part_neigh = jnp.dot(aggregate.T, grad_pre, preferred_element_type=jnp.float32)
    grad_own = jnp.dot(grad_pre, w_self.T, preferred_element_type=jnp.float32)
    grad_agg = (jnp.dot(grad_pre, w_neigh.T, preferred_element_type=jnp.float32) * mean_scale).astype(jnp.bfloat16)
    agg_rows = grad_agg.astype(jnp.float32).reshape(N_GRP, V_DEV, 1, F)
    edge_grads = jnp.broadcast_to(agg_rows, (N_GRP, V_DEV, K, F))
    table_rows = source_table.shape[1]

    def scatter_one(idx, vals):
        return jnp.zeros((table_rows, F), jnp.float32).at[idx.reshape(-1)].add(vals.reshape(-1, F))

    table_grads = jax.vmap(scatter_one)(nbr_part, edge_grads)
    hub_edges = jnp.broadcast_to(agg_rows, (N_GRP, V_DEV, HK, F)).reshape(-1, F)
    hub_grad = jnp.zeros((HUBS, F), jnp.float32).at[hub_part.reshape(-1)].add(hub_edges)
    own_grad = grad_own.reshape(N_GRP, V_DEV, F) + table_grads[:, :V_DEV]
    return hidden, part_self, part_neigh, own_grad, table_grads[:, V_DEV:], hub_grad


def reference(features, hub_features, nbr_ids, hub_ids, halo_rows, w_self, w_neigh, grad_hidden):
    feat_blocks = features.reshape(N_DOM, N_GRP, V_DEV, F)
    halo_blocks = halo_rows.reshape(N_DOM, N_GRP, N_DOM, HALO)
    live_slot = halo_blocks >= 0
    safe_rows = jnp.clip(halo_blocks, 0, V_DEV - 1)
    sent = jax.vmap(jax.vmap(lambda tab, idx: tab[idx]))(feat_blocks, safe_rows)
    sent = jnp.where(live_slot[..., None], sent, jnp.zeros((), jnp.bfloat16))
    received = sent.transpose(2, 1, 0, 3, 4).reshape(N_DOM, N_GRP, N_DOM * HALO, F)
    source_table = jnp.concatenate([feat_blocks, received], axis=2)
    nbr_blocks = nbr_ids.reshape(N_DOM, N_GRP, V_DEV, K)
    hub_blocks = hub_ids.reshape(N_DOM, N_GRP, V_DEV, HK)
    hub_tables = hub_features.reshape(N_DOM, HUBS, F)
    cot_blocks = grad_hidden.reshape(N_DOM, N_GRP, V_DEV, H)

    def per_domain(inputs):
        tab, nbr_part, hub_table, hub_part, own_rows, cot_rows = inputs
        return partition_step(tab, nbr_part, hub_table, hub_part, own_rows, cot_rows, w_self, w_neigh)

    hidden, part_self, part_neigh, own_grad, halo_grad, hub_grad = lax.map(per_domain, (source_table, nbr_blocks, hub_tables, hub_blocks, feat_blocks, cot_blocks))
    back = halo_grad.reshape(N_DOM, N_GRP, N_DOM, HALO, F).transpose(2, 1, 0, 3, 4)
    back = jnp.where(live_slot[..., None], back, 0.0)

    def add_back(base, idx, vals):
        return base.at[idx.reshape(-1)].add(vals.reshape(-1, F))

    grad_features = jax.vmap(jax.vmap(add_back))(own_grad, safe_rows, back)
    return (hidden.reshape(VERTS, H), grad_features.reshape(VERTS, F), hub_grad.reshape(HUB_ALL, F), jnp.sum(part_self, axis=0), jnp.sum(part_neigh, axis=0))
```

```python
import functools

import jax
import jax.numpy as jnp
from jax import lax
from jax.experimental import pallas as pl
from jax.experimental.pallas import tpu as pltpu
from jax.sharding import PartitionSpec as P

K = 12
HK = 4
BF = jnp.bfloat16
F32 = jnp.float32
CONTRACT_ROWS = (((0,), (0,)), ((), ()))
CONTRACT_COLS = (((1,), (1,)), ((), ()))
VMEM = pl.BlockSpec(memory_space=pltpu.VMEM)


def call(kernel, outs, args, flops, limit=24):
    nbytes = sum(a.size * a.dtype.itemsize for a in (*args, *outs))
    return pl.pallas_call(
        kernel,
        out_shape=outs,
        in_specs=[VMEM] * len(args),
        out_specs=[VMEM] * len(outs),
        compiler_params=pltpu.CompilerParams(vmem_limit_bytes=limit * 2**20),
        cost_estimate=pl.CostEstimate(flops=flops, bytes_accessed=nbytes, transcendentals=0),
    )(*args)


def shape(dims, kind):
    return jax.ShapeDtypeStruct(dims, kind)


def pack_kernel(halo_ref, feat_ref, out_ref):
    peers, slots = halo_ref.shape
    rows = feat_ref.shape[0]
    columns = jnp.transpose(halo_ref[...])
    lanes = lax.broadcasted_iota(jnp.int32, (slots, rows), 1)
    for p in range(peers):
        pick = (columns[:, p : p + 1] == lanes).astype(F32).astype(BF)
        out_ref[p] = jnp.dot(pick, feat_ref[...], preferred_element_type=F32).astype(BF)


def add_counts(ids_ref, out_ref, base):
    entries, width = ids_ref.shape
    total = out_ref.shape[0] if base is None else base[1]
    start = 0 if base is None else base[0]
    block = 256
    target = lax.broadcasted_iota(jnp.int32, (block // 16, 16, 128), 0) * 16
    target = target + lax.broadcasted_iota(jnp.int32, (block // 16, 16, 128), 1)
    target = target.astype(F32).astype(BF)
    one, zero = jnp.ones((), BF), jnp.zeros((), BF)

    def body(b, carry):
        for c in range(width // 128):
            ids = ids_ref[:, c * 128 : (c + 1) * 128] - b * block
            inside = (ids >= 0) & (ids < block)
            local = jnp.where(inside, ids, -1).astype(F32)
            acc = jnp.zeros((block // 16, 16, 128), BF)
            for k in range(entries):
                row = jnp.broadcast_to(local[k : k + 1, :], (16, 128)).astype(BF)
                acc = acc + jnp.where(target == row[None], one, zero)
            out_ref[pl.ds(pl.multiple_of(start + b * block, block), block), c * 128 : (c + 1) * 128] = (
                acc.reshape(block, 128)
            )
        return carry

    lax.fori_loop(0, total // block, body, 0)


def count_kernel(nbr_ref, hub_ref, halo_ref, table_ref, hubs_ref, slot_ref):
    add_counts(nbr_ref, table_ref, None)
    add_counts(hub_ref, hubs_ref, None)
    peers, slots = halo_ref.shape
    rows = slot_ref.shape[0]
    sublanes = lax.broadcasted_iota(jnp.int32, (rows, 2 * slots), 0)
    for q in range(peers // 2):
        pair = jnp.concatenate([halo_ref[2 * q : 2 * q + 1, :], halo_ref[2 * q + 1 : 2 * q + 2, :]], axis=1)
        slot_ref[:, 2 * q * slots : (2 * q + 2) * slots] = (sublanes == pair).astype(F32).astype(BF)


def forward_kernel(
    table_ref, hubs_ref, feat_ref, halo_ref, hub_ref, ws_ref, wn_ref, cot_ref,
    hidden_ref, pre_ref, part_ref,
):
    rows = feat_ref.shape[0]
    feat = feat_ref[...]
    agg_t = lax.dot_general(feat, table_ref[:rows, :], CONTRACT_ROWS, preferred_element_type=F32)
    agg_t += lax.dot_general(halo_ref[...], table_ref[rows:, :], CONTRACT_ROWS, preferred_element_type=F32)
    agg_t += lax.dot_general(hub_ref[...], hubs_ref[...], CONTRACT_ROWS, preferred_element_type=F32)
    agg_t = agg_t * (1.0 / (K + HK))
    agg = jnp.transpose(agg_t).astype(BF)
    preact = jnp.dot(feat, ws_ref[...], preferred_element_type=F32)
    preact += jnp.dot(agg, wn_ref[...], preferred_element_type=F32)
    hidden_ref[...] = jnp.maximum(preact, 0.0).astype(BF)
    pre = jnp.where(preact > 0, cot_ref[...].astype(F32), 0.0).astype(BF)
    pre_ref[...] = pre
    part_self = lax.dot_general(feat, pre, CONTRACT_ROWS, preferred_element_type=F32).astype(BF)
    part_neigh = jnp.dot(agg_t.astype(BF), pre, preferred_element_type=F32).astype(BF)
    width = feat.shape[1]
    for i, part in enumerate((part_self, part_neigh)):
        for j in range(2):
            part_ref[(2 * i + j) * width : (2 * i + j + 1) * width, :] = part[:, j * 128 : (j + 1) * 128]


def backward_kernel(table_ref, hubs_ref, pre_ref, ws_ref, wn_ref, hub_ref, halo_ref, own_ref):
    rows = pre_ref.shape[0]
    pre = pre_ref[...]
    grad_agg = lax.dot_general(pre, wn_ref[...], CONTRACT_COLS, preferred_element_type=F32)
    grad_agg = (grad_agg * (1.0 / (K + HK))).astype(BF)
    hub_ref[...] = jnp.dot(hubs_ref[...], grad_agg, preferred_element_type=F32).astype(BF)
    halo_ref[...] = jnp.dot(table_ref[rows:, :], grad_agg, preferred_element_type=F32).astype(BF)
    own = lax.dot_general(pre, ws_ref[...], CONTRACT_COLS, preferred_element_type=F32)
    own_ref[...] = own + jnp.dot(table_ref[:rows, :], grad_agg, preferred_element_type=F32)


def return_kernel(own_ref, slot_ref, back_ref, out_ref):
    out_ref[...] = own_ref[...] + jnp.dot(slot_ref[...], back_ref[...], preferred_element_type=F32)


def sum_kernel(in_ref, out_ref):
    out_ref[...] = jnp.sum(in_ref[...].astype(F32), axis=0)


def spread_kernel(in_ref, out_ref):
    total = jnp.sum(in_ref[...].astype(F32), axis=0)
    out_ref[...] = jnp.broadcast_to(total[None], out_ref.shape).astype(out_ref.dtype)


def weights_kernel(in_ref, self_ref, neigh_ref):
    width = self_ref.shape[0]
    for i, ref in enumerate((self_ref, neigh_ref)):
        for j in range(2):
            ref[:, j * 128 : (j + 1) * 128] = in_ref[(2 * i + j) * width : (2 * i + j + 1) * width, :].astype(F32)


def exchange(value, axis):
    return lax.all_to_all(value, axis, split_axis=0, concat_axis=0, tiled=True)


def on_device(features, hub_features, nbr_ids, hub_ids, halo_rows, w_self, w_neigh, grad_hidden):
    rows, width = features.shape
    hidden_width = w_self.shape[1]
    n_dom = lax.axis_size("dom")
    n_grp = lax.axis_size("grp")
    slots = halo_rows.shape[1]
    hub_local = hub_features.shape[0]
    hubs = hub_local * n_grp
    halo = n_dom * slots

    hub_copies = jnp.broadcast_to(hub_features[None], (n_grp, hub_local, width))
    all_hubs = exchange(hub_copies, "grp").reshape(hubs, width)
    (outgoing,) = call(
        pack_kernel, [shape((n_dom, slots, width), BF)], [halo_rows, features], 2 * halo * rows * width
    )
    incoming = exchange(outgoing, "dom").reshape(halo, width)
    table_counts, hub_counts, slot_pick = call(
        count_kernel,
        [shape((rows + halo, rows), BF), shape((hubs, rows), BF), shape((rows, halo), BF)],
        [nbr_ids.T, hub_ids.T, halo_rows],
        10**9,
    )
    hidden, grad_pre, part = call(
        forward_kernel,
        [shape((rows, hidden_width), BF), shape((rows, hidden_width), BF), shape((4 * width, 128), BF)],
        [table_counts, hub_counts, features, incoming, all_hubs, w_self, w_neigh, grad_hidden],
        2 * rows * width * (rows + halo + hubs + 4 * hidden_width),
    )
    part_rows = 4 * width // n_grp
    got = exchange(part.reshape(n_grp, part_rows, 128), "grp")
    hub_part, halo_part, own = call(
        backward_kernel,
        [shape((hubs, width), BF), shape((halo, width), BF), shape((rows, width), F32)],
        [table_counts, hub_counts, grad_pre, w_self, w_neigh],
        2 * rows * width * (rows + halo + hubs + 2 * hidden_width),
    )
    hub_back = exchange(hub_part.reshape(n_grp, hub_local, width), "grp")
    halo_back = exchange(halo_part.reshape(n_dom, slots, width), "dom")
    (mine,) = call(spread_kernel, [shape((n_dom, part_rows, 128), F32)], [got], 0)
    across = exchange(mine, "dom")
    (total,) = call(spread_kernel, [shape((n_grp, part_rows, 128), F32)], [across], 0)
    whole = exchange(total, "grp").reshape(4 * width, 128)
    grad_w_self, grad_w_neigh = call(
        weights_kernel, [shape((width, hidden_width), F32)] * 2, [whole], 0
    )
    (grad_features,) = call(
        return_kernel,
        [shape((rows, width), F32)],
        [own, slot_pick, halo_back.reshape(halo, width)],
        2 * rows * halo * width,
    )
    (grad_hubs,) = call(sum_kernel, [shape((hub_local, width), F32)], [hub_back], 0)
    return (hidden, grad_features, grad_hubs, grad_w_self, grad_w_neigh)


def solution(mesh):
    both = P(("dom", "grp"), None)
    return jax.shard_map(
        on_device,
        mesh=mesh,
        in_specs=(both, both, both, both, both, P(), P(), both),
        out_specs=(both, both, both, P(), P()),
        check_vma=False,
    )
```

```python
import functools

import jax
import jax.numpy as jnp
from jax import lax
from jax.experimental import pallas as pl
from jax.experimental.pallas import tpu as pltpu
from jax.sharding import PartitionSpec as P

K = 12
HK = 4
BF = jnp.bfloat16
F32 = jnp.float32
CONTRACT_ROWS = (((0,), (0,)), ((), ()))
CONTRACT_COLS = (((1,), (1,)), ((), ()))
VMEM = pl.BlockSpec(memory_space=pltpu.VMEM)
LIMIT = 62


def call(kernel, outs, args, flops, limit=16):
    nbytes = sum(a.size * a.dtype.itemsize for a in (*args, *outs))
    return pl.pallas_call(
        kernel,
        out_shape=outs,
        in_specs=[VMEM] * len(args),
        out_specs=[VMEM] * len(outs),
        compiler_params=pltpu.CompilerParams(vmem_limit_bytes=limit * 2**20),
        cost_estimate=pl.CostEstimate(flops=flops, bytes_accessed=nbytes, transcendentals=0),
    )(*args)


def in_hbm(kernel, outs, args, scratch, flops):
    nbytes = sum(a.size * a.dtype.itemsize for a in (*args, *outs))
    hbm = pl.BlockSpec(memory_space=pltpu.HBM)
    return pl.pallas_call(
        kernel,
        out_shape=outs,
        in_specs=[hbm] * len(args),
        out_specs=[hbm] * len(outs),
        scratch_shapes=scratch,
        compiler_params=pltpu.CompilerParams(vmem_limit_bytes=LIMIT * 2**20),
        cost_estimate=pl.CostEstimate(flops=flops, bytes_accessed=nbytes, transcendentals=0),
    )(*args)


def staged(kernel, outs, args, flops):
    n_in, n_out = len(args), len(outs)

    def body(*refs):
        ins, results, buffers, stages = (
            refs[:n_in],
            refs[n_in : n_in + n_out],
            refs[n_in + n_out : 2 * n_in + n_out],
            refs[2 * n_in + n_out : 2 * (n_in + n_out)],
        )
        in_sem, out_sem = refs[2 * (n_in + n_out) :]
        copies = [pltpu.make_async_copy(ins[n], buffers[n], in_sem.at[n]) for n in range(n_in)]
        for copy in copies:
            copy.start()
        for copy in copies:
            copy.wait()
        kernel(*buffers, *stages)
        copies = [pltpu.make_async_copy(stages[n], results[n], out_sem.at[n]) for n in range(n_out)]
        for copy in copies:
            copy.start()
        for copy in copies:
            copy.wait()

    scratch = [
        *[pltpu.VMEM(a.shape, a.dtype) for a in (*args, *outs)],
        pltpu.SemaphoreType.DMA((n_in,)),
        pltpu.SemaphoreType.DMA((n_out,)),
    ]
    return in_hbm(body, outs, args, scratch, flops)


def shape(dims, kind):
    return jax.ShapeDtypeStruct(dims, kind)


def pack_kernel(halo_ref, feat_ref, out_ref):
    peers, slots = halo_ref.shape
    rows = feat_ref.shape[0]
    columns = jnp.transpose(halo_ref[...])
    lanes = lax.broadcasted_iota(jnp.int32, (slots, rows), 1)
    for p in range(peers):
        pick = (columns[:, p : p + 1] == lanes).astype(F32).astype(BF)
        out_ref[p] = jnp.dot(pick, feat_ref[...], preferred_element_type=F32).astype(BF)


def add_counts(ids_ref, first, out_ref):
    entries, width = ids_ref.shape
    block = 256
    target = lax.broadcasted_iota(jnp.int32, (block // 16, 16, 128), 0) * 16
    target = target + lax.broadcasted_iota(jnp.int32, (block // 16, 16, 128), 1)
    target = target.astype(F32).astype(BF)
    one, zero = jnp.ones((), BF), jnp.zeros((), BF)

    def body(b, carry):
        for c in range(width // 128):
            ids = ids_ref[:, c * 128 : (c + 1) * 128] - (first + b * block)
            inside = (ids >= 0) & (ids < block)
            local = jnp.where(inside, ids, -1).astype(F32)
            acc = jnp.zeros((block // 16, 16, 128), BF)
            for k in range(entries):
                row = jnp.broadcast_to(local[k : k + 1, :], (16, 128)).astype(BF)
                acc = acc + jnp.where(target == row[None], one, zero)
            out_ref[pl.ds(pl.multiple_of(b * block, block), block), c * 128 : (c + 1) * 128] = (
                acc.reshape(block, 128)
            )
        return carry

    lax.fori_loop(0, out_ref.shape[0] // block, body, 0)


def count_kernel(nbr_ref, hub_ref, halo_ref, own_ref, in_ref, hubs_ref, slot_ref):
    add_counts(nbr_ref, 0, own_ref)
    add_counts(nbr_ref, own_ref.shape[0], in_ref)
    add_counts(hub_ref, 0, hubs_ref)
    peers, slots = halo_ref.shape
    rows = slot_ref.shape[0]
    sublanes = lax.broadcasted_iota(jnp.int32, (rows, 2 * slots), 0)
    for q in range(peers // 2):
        pair = jnp.concatenate([halo_ref[2 * q : 2 * q + 1, :], halo_ref[2 * q + 1 : 2 * q + 2, :]], axis=1)
        slot_ref[:, 2 * q * slots : (2 * q + 2) * slots] = (sublanes == pair).astype(F32).astype(BF)


def copies_kernel(hub_ref, out_ref):
    out_ref[...] = jnp.broadcast_to(hub_ref[...][None], out_ref.shape)


def hub_kernel(hubs_ref, hub_ref, feat_ref, ws_ref, own_ref, agg_ref, pre_ref):
    agg_t = lax.dot_general(hub_ref[...], hubs_ref[...], CONTRACT_ROWS, preferred_element_type=F32)
    agg_ref[...] = agg_t + lax.dot_general(feat_ref[...], own_ref[...], CONTRACT_ROWS, preferred_element_type=F32)
    pre_ref[...] = jnp.dot(feat_ref[...], ws_ref[...], preferred_element_type=F32)


CHUNKS = 4


def forward_kernel(
    halo_ref, feat_ref, counts_ref, agg_ref, self_ref, wn_ref, cot_ref, hubs_ref,
    hidden_ref, pre_ref, grad_ref, send_ref,
    halo_in, feat_in, counts_in, agg_in, self_in, wn_in, cot_in, hubs_in,
    hidden_out, pre_out, grad_out, send_out,
    in_sem, hub_sem, out_sem, send_sem,
):
    loads = [
        pltpu.make_async_copy(source, target, in_sem.at[n])
        for n, (source, target) in enumerate(
            (
                (halo_ref, halo_in),
                (counts_ref, counts_in),
                (agg_ref, agg_in),
                (wn_ref, wn_in),
                (self_ref, self_in),
                (cot_ref, cot_in),
                (feat_ref, feat_in),
            )
        )
    ]
    n_grp, send_rows = send_ref.shape[:2]
    hubs = hubs_ref.shape[0]
    hub_local = hubs // n_grp
    part_rows = send_rows - hub_local
    step, peers = hubs // CHUNKS, n_grp // CHUNKS
    hub_loads = [
        pltpu.make_async_copy(
            hubs_ref.at[pl.ds(c * step, step)], hubs_in.at[pl.ds(c * step, step)], hub_sem.at[c]
        )
        for c in range(CHUNKS)
    ]
    sends = [
        pltpu.make_async_copy(
            send_out.at[pl.ds(c * peers, peers)], send_ref.at[pl.ds(c * peers, peers)], send_sem.at[c]
        )
        for c in range(CHUNKS)
    ]
    backs = [
        pltpu.make_async_copy(source, target, out_sem.at[n])
        for n, (source, target) in enumerate(
            ((hidden_out, hidden_ref), (pre_out, pre_ref), (grad_out, grad_ref))
        )
    ]
    for copy in (*loads, *hub_loads):
        copy.start()
    loads[0].wait()
    loads[1].wait()
    agg_t = lax.dot_general(halo_in[...], counts_in[...], CONTRACT_ROWS, preferred_element_type=F32)
    loads[2].wait()
    agg_t = (agg_t + agg_in[...]) * (1.0 / (K + HK))
    agg = jnp.transpose(agg_t).astype(BF)
    loads[3].wait()
    loads[4].wait()
    preact = self_in[...] + jnp.dot(agg, wn_in[...], preferred_element_type=F32)
    hidden_out[...] = jnp.maximum(preact, 0.0).astype(BF)
    backs[0].start()
    loads[5].wait()
    pre = jnp.where(preact > 0, cot_in[...].astype(F32), 0.0).astype(BF)
    pre_out[...] = pre
    backs[1].start()
    grad_agg = lax.dot_general(pre, wn_in[...], CONTRACT_COLS, preferred_element_type=F32)
    grad_agg = (grad_agg * (1.0 / (K + HK))).astype(BF)
    grad_out[...] = grad_agg
    backs[2].start()
    loads[6].wait()
    part_self = lax.dot_general(feat_in[...], pre, CONTRACT_ROWS, preferred_element_type=F32)
    part_neigh = jnp.dot(agg_t.astype(BF), pre, preferred_element_type=F32)
    part = jnp.concatenate(
        [part_self[:, :128], part_self[:, 128:], part_neigh[:, :128], part_neigh[:, 128:]], axis=0
    )
    for c in range(CHUNKS):
        hub_loads[c].wait()
        hub_part = jnp.dot(
            hubs_in[c * step : (c + 1) * step, :], grad_agg, preferred_element_type=F32
        )
        for i in range(peers):
            g = c * peers + i
            both = [hub_part[i * hub_local : (i + 1) * hub_local], part[g * part_rows : (g + 1) * part_rows]]
            send_out[g] = jnp.concatenate(both, axis=0).astype(BF)
        sends[c].start()
    for copy in (*backs, *sends):
        copy.wait()


def backward_kernel(own_counts_ref, counts_ref, pre_ref, grad_ref, ws_ref, halo_ref, own_ref):
    slots = halo_ref.shape[1]
    grad_agg = grad_ref[...]
    halo = jnp.dot(counts_ref[...], grad_agg, preferred_element_type=F32)
    for p in range(halo_ref.shape[0]):
        halo_ref[p] = halo[p * slots : (p + 1) * slots].astype(BF)
    own = lax.dot_general(pre_ref[...], ws_ref[...], CONTRACT_COLS, preferred_element_type=F32)
    own_ref[...] = own + jnp.dot(own_counts_ref[...], grad_agg, preferred_element_type=F32)


def total(in_ref, first, last):
    acc = in_ref[0].astype(F32)[first:last]
    for i in range(1, in_ref.shape[0]):
        acc = acc + in_ref[i].astype(F32)[first:last]
    return acc


def second_kernel(got_ref, halo_ref, send_ref):
    peers, slots = halo_ref.shape[:2]
    part_rows = send_ref.shape[1] - slots
    hub_local = got_ref.shape[1] - part_rows
    part = total(got_ref, hub_local, hub_local + part_rows)
    for p in range(peers):
        send_ref[p] = jnp.concatenate([halo_ref[p].astype(F32), part], axis=0).astype(BF)


def hub_sum_kernel(got_ref, out_ref):
    out_ref[...] = total(got_ref, 0, out_ref.shape[0])


def third_kernel(got_ref, out_ref):
    part_rows = out_ref.shape[1]
    slots = got_ref.shape[1] - part_rows
    part = total(got_ref, slots, slots + part_rows).astype(BF)
    out_ref[...] = jnp.broadcast_to(part[None], out_ref.shape)


def return_kernel(own_ref, slot_ref, got_ref, out_ref):
    peers = got_ref.shape[0]
    slots = slot_ref.shape[1] // peers
    back = jnp.concatenate([got_ref[p].astype(F32)[:slots] for p in range(peers)], axis=0).astype(BF)
    out_ref[...] = own_ref[...] + jnp.dot(slot_ref[...], back, preferred_element_type=F32)


def weights_kernel(in_ref, self_ref, neigh_ref):
    width = self_ref.shape[0]
    for i, ref in enumerate((self_ref, neigh_ref)):
        for j in range(2):
            ref[:, j * 128 : (j + 1) * 128] = in_ref[(2 * i + j) * width : (2 * i + j + 1) * width, :].astype(F32)


def exchange(value, axis):
    return lax.all_to_all(value, axis, split_axis=0, concat_axis=0, tiled=True)


def on_device(features, hub_features, nbr_ids, hub_ids, halo_rows, w_self, w_neigh, grad_hidden):
    rows, width = features.shape
    hidden_width = w_self.shape[1]
    n_dom = lax.axis_size("dom")
    n_grp = lax.axis_size("grp")
    slots = halo_rows.shape[1]
    hub_local = hub_features.shape[0]
    hubs = hub_local * n_grp
    halo = n_dom * slots

    part_rows = 4 * width // n_grp

    (hub_copies,) = call(copies_kernel, [shape((n_grp, hub_local, width), BF)], [hub_features], 0)
    all_hubs = exchange(hub_copies, "grp").reshape(hubs, width)
    (outgoing,) = staged(
        pack_kernel, [shape((n_dom, slots, width), BF)], [halo_rows, features], 2 * halo * rows * width
    )
    own_counts, halo_counts, hub_counts, slot_pick = staged(
        count_kernel,
        [shape((rows, rows), BF), shape((halo, rows), BF), shape((hubs, rows), BF), shape((rows, halo), BF)],
        [nbr_ids.T, hub_ids.T, halo_rows],
        10**9,
    )
    outgoing, all_hubs, own_counts, halo_counts, hub_counts, slot_pick = lax.optimization_barrier(
        (outgoing, all_hubs, own_counts, halo_counts, hub_counts, slot_pick)
    )
    incoming = exchange(outgoing, "dom").reshape(halo, width)
    agg_part, pre_self = staged(
        hub_kernel,
        [shape((width, rows), F32), shape((rows, hidden_width), F32)],
        [hub_counts, all_hubs, features, w_self, own_counts],
        2 * rows * width * (hubs + rows + hidden_width),
    )
    forward_args = [incoming, features, halo_counts, agg_part, pre_self, w_neigh, grad_hidden, hub_counts]
    forward_outs = [
        shape((rows, hidden_width), BF),
        shape((rows, hidden_width), BF),
        shape((rows, width), BF),
        shape((n_grp, hub_local + part_rows, width), BF),
    ]
    hidden, grad_pre, grad_agg, send = in_hbm(
        forward_kernel,
        forward_outs,
        forward_args,
        [
            *[pltpu.VMEM(a.shape, a.dtype) for a in (*forward_args, *forward_outs)],
            pltpu.SemaphoreType.DMA((7,)),
            pltpu.SemaphoreType.DMA((CHUNKS,)),
            pltpu.SemaphoreType.DMA((3,)),
            pltpu.SemaphoreType.DMA((CHUNKS,)),
        ],
        2 * rows * width * (halo + hubs + 4 * hidden_width),
    )
    got = exchange(send, "grp")
    halo_part, own = call(
        backward_kernel,
        [shape((n_dom, slots, width), BF), shape((rows, width), F32)],
        [own_counts, halo_counts, grad_pre, grad_agg, w_self],
        2 * rows * width * (rows + halo + hidden_width),
    )
    (send,) = call(second_kernel, [shape((n_dom, slots + part_rows, width), BF)], [got, halo_part], 0)
    back = exchange(send, "dom")
    (grad_hubs,) = call(hub_sum_kernel, [shape((hub_local, width), F32)], [got], 0)
    (send,) = call(third_kernel, [shape((n_grp, part_rows, width), BF)], [back], 0)
    whole = exchange(send, "grp").reshape(4 * width, width)
    (grad_features,) = call(
        return_kernel, [shape((rows, width), F32)], [own, slot_pick, back], 2 * rows * halo * width
    )
    grad_w_self, grad_w_neigh = call(
        weights_kernel, [shape((width, hidden_width), F32)] * 2, [whole], 0
    )
    return (hidden, grad_features, grad_hubs, grad_w_self, grad_w_neigh)


def solution(mesh):
    both = P(("dom", "grp"), None)
    return jax.shard_map(
        on_device,
        mesh=mesh,
        in_specs=(both, both, both, both, both, P(), P(), both),
        out_specs=(both, both, both, P(), P()),
        check_vma=False,
    )
```

```python
import functools

import jax
import jax.numpy as jnp
from jax import lax
from jax.experimental import pallas as pl
from jax.experimental.pallas import tpu as pltpu
from jax.sharding import PartitionSpec as P

K = 12
HK = 4
BF = jnp.bfloat16
F32 = jnp.float32
I8 = jnp.int8
CONTRACT_ROWS = (((0,), (0,)), ((), ()))
CONTRACT_COLS = (((1,), (1,)), ((), ()))
VMEM = pl.BlockSpec(memory_space=pltpu.VMEM)
LIMIT = 53


def call(kernel, outs, args, flops, limit=16):
    nbytes = sum(a.size * a.dtype.itemsize for a in (*args, *outs))
    return pl.pallas_call(
        kernel,
        out_shape=outs,
        in_specs=[VMEM] * len(args),
        out_specs=[VMEM] * len(outs),
        compiler_params=pltpu.CompilerParams(vmem_limit_bytes=limit * 2**20),
        cost_estimate=pl.CostEstimate(flops=flops, bytes_accessed=nbytes, transcendentals=0),
    )(*args)


def in_hbm(kernel, outs, args, scratch, flops):
    nbytes = sum(a.size * a.dtype.itemsize for a in (*args, *outs))
    hbm = pl.BlockSpec(memory_space=pltpu.HBM)
    return pl.pallas_call(
        kernel,
        out_shape=outs,
        in_specs=[hbm] * len(args),
        out_specs=[hbm] * len(outs),
        scratch_shapes=scratch,
        compiler_params=pltpu.CompilerParams(vmem_limit_bytes=LIMIT * 2**20),
        cost_estimate=pl.CostEstimate(flops=flops, bytes_accessed=nbytes, transcendentals=0),
    )(*args)


def staged(kernel, outs, args, flops):
    n_in, n_out = len(args), len(outs)

    def body(*refs):
        ins, results, buffers, stages = (
            refs[:n_in],
            refs[n_in : n_in + n_out],
            refs[n_in + n_out : 2 * n_in + n_out],
            refs[2 * n_in + n_out : 2 * (n_in + n_out)],
        )
        in_sem, out_sem = refs[2 * (n_in + n_out) :]
        copies = [pltpu.make_async_copy(ins[n], buffers[n], in_sem.at[n]) for n in range(n_in)]
        for copy in copies:
            copy.start()
        for copy in copies:
            copy.wait()
        kernel(*buffers, *stages)
        copies = [pltpu.make_async_copy(stages[n], results[n], out_sem.at[n]) for n in range(n_out)]
        for copy in copies:
            copy.start()
        for copy in copies:
            copy.wait()

    scratch = [
        *[pltpu.VMEM(a.shape, a.dtype) for a in (*args, *outs)],
        pltpu.SemaphoreType.DMA((n_in,)),
        pltpu.SemaphoreType.DMA((n_out,)),
    ]
    return in_hbm(body, outs, args, scratch, flops)


def shape(dims, kind):
    return jax.ShapeDtypeStruct(dims, kind)


def pack_kernel(halo_ref, feat_ref, out_ref):
    peers, slots = halo_ref.shape
    rows = feat_ref.shape[0]
    columns = jnp.transpose(halo_ref[...])
    lanes = lax.broadcasted_iota(jnp.int32, (slots, rows), 1)
    for p in range(peers):
        pick = (columns[:, p : p + 1] == lanes).astype(F32).astype(BF)
        out_ref[p] = jnp.dot(pick, feat_ref[...], preferred_element_type=F32).astype(BF)


def add_counts(ids_ref, first, out_ref):
    entries, width = ids_ref.shape
    block = 256
    target = lax.broadcasted_iota(jnp.int32, (block // 16, 16, 128), 0) * 16
    target = target + lax.broadcasted_iota(jnp.int32, (block // 16, 16, 128), 1)
    target = target.astype(F32).astype(BF)
    one, zero = jnp.ones((), BF), jnp.zeros((), BF)

    def body(b, carry):
        for c in range(width // 128):
            ids = ids_ref[:, c * 128 : (c + 1) * 128] - (first + b * block)
            inside = (ids >= 0) & (ids < block)
            local = jnp.where(inside, ids, -1).astype(F32)
            acc = jnp.zeros((block // 16, 16, 128), BF)
            for k in range(entries):
                row = jnp.broadcast_to(local[k : k + 1, :], (16, 128)).astype(BF)
                acc = acc + jnp.where(target == row[None], one, zero)
            out_ref[pl.ds(pl.multiple_of(b * block, block), block), c * 128 : (c + 1) * 128] = (
                acc.reshape(block, 128).astype(I8)
            )
        return carry

    lax.fori_loop(0, out_ref.shape[0] // block, body, 0)


def count_kernel(nbr_ref, hub_ref, halo_ref, own_ref, in_ref, hubs_ref, slot_ref):
    add_counts(nbr_ref, 0, own_ref)
    add_counts(nbr_ref, own_ref.shape[0], in_ref)
    add_counts(hub_ref, 0, hubs_ref)
    peers, slots = halo_ref.shape
    rows = slot_ref.shape[0]
    sublanes = lax.broadcasted_iota(jnp.int32, (rows, 2 * slots), 0)
    for q in range(peers // 2):
        pair = jnp.concatenate([halo_ref[2 * q : 2 * q + 1, :], halo_ref[2 * q + 1 : 2 * q + 2, :]], axis=1)
        slot_ref[:, 2 * q * slots : (2 * q + 2) * slots] = (sublanes == pair).astype(F32).astype(BF)


def copies_kernel(hub_ref, out_ref):
    out_ref[...] = jnp.broadcast_to(hub_ref[...][None], out_ref.shape)


def hub_kernel(hubs_ref, hub_ref, feat_ref, own_ref, agg_ref):
    agg_t = lax.dot_general(hub_ref[...], hubs_ref[...].astype(BF), CONTRACT_ROWS, preferred_element_type=F32)
    agg_ref[...] = agg_t + lax.dot_general(
        feat_ref[...], own_ref[...].astype(BF), CONTRACT_ROWS, preferred_element_type=F32
    )


CHUNKS = 4


def forward_kernel(
    halo_ref, feat_ref, counts_ref, agg_ref, ws_ref, wn_ref, cot_ref, hubs_ref,
    hidden_ref, pre_ref, grad_ref, send_ref,
    halo_in, feat_in, counts_in, agg_in, ws_in, wn_in, cot_in, hubs_in,
    hidden_out, pre_out, grad_out, send_out,
    in_sem, hub_sem, out_sem, send_sem,
):
    pairs = (
        (feat_ref, feat_in),
        (ws_ref, ws_in),
        (halo_ref, halo_in),
        (counts_ref, counts_in),
        (agg_ref, agg_in),
        (wn_ref, wn_in),
        (cot_ref, cot_in),
    )
    feat_load, ws_load, halo_load, counts_load, agg_load, wn_load, cot_load = loads = [
        pltpu.make_async_copy(source, target, in_sem.at[n]) for n, (source, target) in enumerate(pairs)
    ]
    n_grp, send_rows = send_ref.shape[:2]
    hubs = hubs_ref.shape[0]
    hub_local = hubs // n_grp
    part_rows = send_rows - hub_local
    step, peers = hubs // CHUNKS, n_grp // CHUNKS
    hub_loads = [
        pltpu.make_async_copy(
            hubs_ref.at[pl.ds(c * step, step)], hubs_in.at[pl.ds(c * step, step)], hub_sem.at[c]
        )
        for c in range(CHUNKS)
    ]
    sends = [
        pltpu.make_async_copy(
            send_out.at[pl.ds(c * peers, peers)], send_ref.at[pl.ds(c * peers, peers)], send_sem.at[c]
        )
        for c in range(CHUNKS)
    ]
    backs = [
        pltpu.make_async_copy(source, target, out_sem.at[n])
        for n, (source, target) in enumerate(
            ((hidden_out, hidden_ref), (pre_out, pre_ref), (grad_out, grad_ref))
        )
    ]
    for copy in loads:
        copy.start()
    for copy in loads:
        copy.wait()
    for copy in hub_loads:
        copy.start()
    preact = jnp.dot(feat_in[...], ws_in[...], preferred_element_type=F32)
    agg_t = lax.dot_general(halo_in[...], counts_in[...].astype(BF), CONTRACT_ROWS, preferred_element_type=F32)
    agg_t = (agg_t + agg_in[...]) * (1.0 / (K + HK))
    agg = jnp.transpose(agg_t).astype(BF)
    preact += jnp.dot(agg, wn_in[...], preferred_element_type=F32)
    hidden_out[...] = jnp.maximum(preact, 0.0).astype(BF)
    pre = jnp.where(preact > 0, cot_in[...].astype(F32), 0.0).astype(BF)
    pre_out[...] = pre
    grad_agg = lax.dot_general(pre, wn_in[...], CONTRACT_COLS, preferred_element_type=F32)
    grad_agg = (grad_agg * (1.0 / (K + HK))).astype(BF)
    grad_out[...] = grad_agg
    part_self = lax.dot_general(feat_in[...], pre, CONTRACT_ROWS, preferred_element_type=F32)
    part_neigh = jnp.dot(agg_t.astype(BF), pre, preferred_element_type=F32)
    part = jnp.concatenate(
        [part_self[:, :128], part_self[:, 128:], part_neigh[:, :128], part_neigh[:, 128:]], axis=0
    )
    for copy in backs:
        copy.start()
    for copy in hub_loads:
        copy.wait()
    for c in range(CHUNKS):
        hub_part = jnp.dot(
            hubs_in[c * step : (c + 1) * step, :].astype(BF), grad_agg, preferred_element_type=F32
        )
        for i in range(peers):
            g = c * peers + i
            both = [hub_part[i * hub_local : (i + 1) * hub_local], part[g * part_rows : (g + 1) * part_rows]]
            send_out[g] = jnp.concatenate(both, axis=0).astype(BF)
    for copy in sends:
        copy.start()
    for copy in (*backs, *sends):
        copy.wait()


def backward_kernel(own_counts_ref, counts_ref, pre_ref, grad_ref, ws_ref, halo_ref, own_ref):
    slots = halo_ref.shape[1]
    grad_agg = grad_ref[...]
    halo = jnp.dot(counts_ref[...].astype(BF), grad_agg, preferred_element_type=F32)
    for p in range(halo_ref.shape[0]):
        halo_ref[p] = halo[p * slots : (p + 1) * slots].astype(BF)
    own = lax.dot_general(pre_ref[...], ws_ref[...], CONTRACT_COLS, preferred_element_type=F32)
    own_ref[...] = own + jnp.dot(own_counts_ref[...].astype(BF), grad_agg, preferred_element_type=F32)


def total(in_ref, first, last):
    acc = in_ref[0].astype(F32)[first:last]
    for i in range(1, in_ref.shape[0]):
        acc = acc + in_ref[i].astype(F32)[first:last]
    return acc


def second_kernel(got_ref, halo_ref, send_ref):
    peers, slots = halo_ref.shape[:2]
    part_rows = send_ref.shape[1] - slots
    hub_local = got_ref.shape[1] - part_rows
    part = total(got_ref, hub_local, hub_local + part_rows)
    for p in range(peers):
        send_ref[p] = jnp.concatenate([halo_ref[p].astype(F32), part], axis=0).astype(BF)


def hub_sum_kernel(got_ref, out_ref):
    out_ref[...] = total(got_ref, 0, out_ref.shape[0])


def third_kernel(got_ref, out_ref):
    part_rows = out_ref.shape[1]
    slots = got_ref.shape[1] - part_rows
    part = total(got_ref, slots, slots + part_rows).astype(BF)
    out_ref[...] = jnp.broadcast_to(part[None], out_ref.shape)


def return_kernel(own_ref, slot_ref, got_ref, out_ref):
    peers = got_ref.shape[0]
    slots = slot_ref.shape[1] // peers
    back = jnp.concatenate([got_ref[p].astype(F32)[:slots] for p in range(peers)], axis=0).astype(BF)
    out_ref[...] = own_ref[...] + jnp.dot(slot_ref[...], back, preferred_element_type=F32)


def weights_kernel(in_ref, self_ref, neigh_ref):
    width = self_ref.shape[0]
    for i, ref in enumerate((self_ref, neigh_ref)):
        for j in range(2):
            ref[:, j * 128 : (j + 1) * 128] = in_ref[(2 * i + j) * width : (2 * i + j + 1) * width, :].astype(F32)


def exchange(value, axis):
    return lax.all_to_all(value, axis, split_axis=0, concat_axis=0, tiled=True)


def on_device(features, hub_features, nbr_ids, hub_ids, halo_rows, w_self, w_neigh, grad_hidden):
    rows, width = features.shape
    hidden_width = w_self.shape[1]
    n_dom = lax.axis_size("dom")
    n_grp = lax.axis_size("grp")
    slots = halo_rows.shape[1]
    hub_local = hub_features.shape[0]
    hubs = hub_local * n_grp
    halo = n_dom * slots

    part_rows = 4 * width // n_grp

    (hub_copies,) = staged(copies_kernel, [shape((n_grp, hub_local, width), BF)], [hub_features], 0)
    all_hubs = exchange(hub_copies, "grp").reshape(hubs, width)
    (outgoing,) = staged(
        pack_kernel, [shape((n_dom, slots, width), BF)], [halo_rows, features], 2 * halo * rows * width
    )
    own_counts, halo_counts, hub_counts, slot_pick = staged(
        count_kernel,
        [shape((rows, rows), I8), shape((halo, rows), I8), shape((hubs, rows), I8), shape((rows, halo), BF)],
        [nbr_ids.T, hub_ids.T, halo_rows],
        10**9,
    )
    outgoing, all_hubs, own_counts, halo_counts, hub_counts, slot_pick = lax.optimization_barrier(
        (outgoing, all_hubs, own_counts, halo_counts, hub_counts, slot_pick)
    )
    incoming = exchange(outgoing, "dom").reshape(halo, width)
    (agg_part,) = staged(
        hub_kernel,
        [shape((width, rows), F32)],
        [hub_counts, all_hubs, features, own_counts],
        2 * rows * width * (hubs + rows),
    )
    forward_args = [incoming, features, halo_counts, agg_part, w_self, w_neigh, grad_hidden, hub_counts]
    forward_outs = [
        shape((rows, hidden_width), BF),
        shape((rows, hidden_width), BF),
        shape((rows, width), BF),
        shape((n_grp, hub_local + part_rows, width), BF),
    ]
    hidden, grad_pre, grad_agg, send = in_hbm(
        forward_kernel,
        forward_outs,
        forward_args,
        [
            *[pltpu.VMEM(a.shape, a.dtype) for a in (*forward_args, *forward_outs)],
            pltpu.SemaphoreType.DMA((7,)),
            pltpu.SemaphoreType.DMA((CHUNKS,)),
            pltpu.SemaphoreType.DMA((3,)),
            pltpu.SemaphoreType.DMA((CHUNKS,)),
        ],
        2 * rows * width * (halo + hubs + 4 * hidden_width),
    )
    got = exchange(send, "grp")
    halo_part, own = call(
        backward_kernel,
        [shape((n_dom, slots, width), BF), shape((rows, width), F32)],
        [own_counts, halo_counts, grad_pre, grad_agg, w_self],
        2 * rows * width * (rows + halo + hidden_width),
    )
    (send,) = call(second_kernel, [shape((n_dom, slots + part_rows, width), BF)], [got, halo_part], 0)
    back = exchange(send, "dom")
    (grad_hubs,) = call(hub_sum_kernel, [shape((hub_local, width), F32)], [got], 0)
    (send,) = call(third_kernel, [shape((n_grp, part_rows, width), BF)], [back], 0)
    whole = exchange(send, "grp").reshape(4 * width, width)
    (grad_features,) = call(
        return_kernel, [shape((rows, width), F32)], [own, slot_pick, back], 2 * rows * halo * width
    )
    grad_w_self, grad_w_neigh = call(
        weights_kernel, [shape((width, hidden_width), F32)] * 2, [whole], 0
    )
    return (hidden, grad_features, grad_hubs, grad_w_self, grad_w_neigh)


def solution(mesh):
    both = P(("dom", "grp"), None)
    return jax.shard_map(
        on_device,
        mesh=mesh,
        in_specs=(both, both, both, both, both, P(), P(), both),
        out_specs=(both, both, both, P(), P()),
        check_vma=False,
    )
```

```python
import functools

import jax
import jax.numpy as jnp
from jax import lax
from jax.experimental import pallas as pl
from jax.experimental.pallas import tpu as pltpu
from jax.sharding import PartitionSpec as P

K = 12
HK = 4
BF = jnp.bfloat16
F32 = jnp.float32
I8 = jnp.int8
CONTRACT_ROWS = (((0,), (0,)), ((), ()))
CONTRACT_COLS = (((1,), (1,)), ((), ()))
VMEM = pl.BlockSpec(memory_space=pltpu.VMEM)
LIMIT = 52


def call(kernel, outs, args, flops, limit=16):
    nbytes = sum(a.size * a.dtype.itemsize for a in (*args, *outs))
    return pl.pallas_call(
        kernel,
        out_shape=outs,
        in_specs=[VMEM] * len(args),
        out_specs=[VMEM] * len(outs),
        compiler_params=pltpu.CompilerParams(vmem_limit_bytes=limit * 2**20),
        cost_estimate=pl.CostEstimate(flops=flops, bytes_accessed=nbytes, transcendentals=0),
    )(*args)


def in_hbm(kernel, outs, args, scratch, flops):
    nbytes = sum(a.size * a.dtype.itemsize for a in (*args, *outs))
    hbm = pl.BlockSpec(memory_space=pltpu.HBM)
    return pl.pallas_call(
        kernel,
        out_shape=outs,
        in_specs=[hbm] * len(args),
        out_specs=[hbm] * len(outs),
        scratch_shapes=scratch,
        compiler_params=pltpu.CompilerParams(vmem_limit_bytes=LIMIT * 2**20),
        cost_estimate=pl.CostEstimate(flops=flops, bytes_accessed=nbytes, transcendentals=0),
    )(*args)


def staged(kernel, outs, args, flops):
    n_in, n_out = len(args), len(outs)

    def body(*refs):
        ins, results, buffers, stages = (
            refs[:n_in],
            refs[n_in : n_in + n_out],
            refs[n_in + n_out : 2 * n_in + n_out],
            refs[2 * n_in + n_out : 2 * (n_in + n_out)],
        )
        in_sem, out_sem = refs[2 * (n_in + n_out) :]
        copies = [pltpu.make_async_copy(ins[n], buffers[n], in_sem.at[n]) for n in range(n_in)]
        for copy in copies:
            copy.start()
        for copy in copies:
            copy.wait()
        kernel(*buffers, *stages)
        copies = [pltpu.make_async_copy(stages[n], results[n], out_sem.at[n]) for n in range(n_out)]
        for copy in copies:
            copy.start()
        for copy in copies:
            copy.wait()

    scratch = [
        *[pltpu.VMEM(a.shape, a.dtype) for a in (*args, *outs)],
        pltpu.SemaphoreType.DMA((n_in,)),
        pltpu.SemaphoreType.DMA((n_out,)),
    ]
    return in_hbm(body, outs, args, scratch, flops)


def shape(dims, kind):
    return jax.ShapeDtypeStruct(dims, kind)


def pack_kernel(halo_ref, feat_ref, out_ref):
    peers, slots = halo_ref.shape
    rows = feat_ref.shape[0]
    columns = jnp.transpose(halo_ref[...])
    lanes = lax.broadcasted_iota(jnp.int32, (slots, rows), 1)
    for p in range(peers):
        pick = (columns[:, p : p + 1] == lanes).astype(F32).astype(BF)
        out_ref[p] = jnp.dot(pick, feat_ref[...], preferred_element_type=F32).astype(BF)


def add_counts(ids_ref, first, out_ref):
    entries, width = ids_ref.shape
    block = 256
    target = lax.broadcasted_iota(jnp.int32, (block // 16, 16, 128), 0) * 16
    target = target + lax.broadcasted_iota(jnp.int32, (block // 16, 16, 128), 1)
    target = target.astype(F32).astype(BF)
    one, zero = jnp.ones((), BF), jnp.zeros((), BF)

    def body(b, carry):
        for c in range(width // 128):
            ids = ids_ref[:, c * 128 : (c + 1) * 128] - (first + b * block)
            inside = (ids >= 0) & (ids < block)
            local = jnp.where(inside, ids, -1).astype(F32)
            acc = jnp.zeros((block // 16, 16, 128), BF)
            for k in range(entries):
                row = jnp.broadcast_to(local[k : k + 1, :], (16, 128)).astype(BF)
                acc = acc + jnp.where(target == row[None], one, zero)
            out_ref[pl.ds(pl.multiple_of(b * block, block), block), c * 128 : (c + 1) * 128] = (
                acc.reshape(block, 128).astype(I8)
            )
        return carry

    lax.fori_loop(0, out_ref.shape[0] // block, body, 0)


def count_kernel(nbr_ref, hub_ref, halo_ref, own_ref, in_ref, hubs_ref, slot_ref):
    add_counts(nbr_ref, 0, own_ref)
    add_counts(nbr_ref, own_ref.shape[0], in_ref)
    add_counts(hub_ref, 0, hubs_ref)
    peers, slots = halo_ref.shape
    rows = slot_ref.shape[0]
    sublanes = lax.broadcasted_iota(jnp.int32, (rows, 2 * slots), 0)
    for q in range(peers // 2):
        pair = jnp.concatenate([halo_ref[2 * q : 2 * q + 1, :], halo_ref[2 * q + 1 : 2 * q + 2, :]], axis=1)
        slot_ref[:, 2 * q * slots : (2 * q + 2) * slots] = (sublanes == pair).astype(F32).astype(BF)


def copies_kernel(hub_ref, out_ref):
    out_ref[...] = jnp.broadcast_to(hub_ref[...][None], out_ref.shape)


def hub_kernel(hubs_ref, hub_ref, feat_ref, own_ref, agg_ref):
    agg_t = lax.dot_general(hub_ref[...], hubs_ref[...].astype(BF), CONTRACT_ROWS, preferred_element_type=F32)
    agg_ref[...] = agg_t + lax.dot_general(
        feat_ref[...], own_ref[...].astype(BF), CONTRACT_ROWS, preferred_element_type=F32
    )


def forward_kernel(
    halo_ref, feat_ref, counts_ref, agg_ref, ws_ref, wn_ref, cot_ref,
    hidden_ref, pre_ref, grad_ref, send_ref,
):
    feat = feat_ref[...]
    n_grp, part_rows = send_ref.shape[:2]
    preact = jnp.dot(feat, ws_ref[...], preferred_element_type=F32)
    agg_t = lax.dot_general(halo_ref[...], counts_ref[...].astype(BF), CONTRACT_ROWS, preferred_element_type=F32)
    agg_t = (agg_t + agg_ref[...]) * (1.0 / (K + HK))
    agg = jnp.transpose(agg_t).astype(BF)
    preact += jnp.dot(agg, wn_ref[...], preferred_element_type=F32)
    hidden_ref[...] = jnp.maximum(preact, 0.0).astype(BF)
    pre = jnp.where(preact > 0, cot_ref[...].astype(F32), 0.0).astype(BF)
    pre_ref[...] = pre
    grad_agg = lax.dot_general(pre, wn_ref[...], CONTRACT_COLS, preferred_element_type=F32)
    grad_ref[...] = (grad_agg * (1.0 / (K + HK))).astype(BF)
    part_self = lax.dot_general(feat, pre, CONTRACT_ROWS, preferred_element_type=F32)
    part_neigh = jnp.dot(agg_t.astype(BF), pre, preferred_element_type=F32)
    part = jnp.concatenate(
        [part_self[:, :128], part_self[:, 128:], part_neigh[:, :128], part_neigh[:, 128:]], axis=0
    )
    for g in range(n_grp):
        send_ref[g] = part[g * part_rows : (g + 1) * part_rows].astype(BF)


def backward_kernel(own_counts_ref, counts_ref, hubs_ref, pre_ref, grad_ref, ws_ref, halo_ref, own_ref, hub_ref):
    slots = halo_ref.shape[1]
    grad_agg = grad_ref[...]
    halo = jnp.dot(counts_ref[...].astype(BF), grad_agg, preferred_element_type=F32)
    for p in range(halo_ref.shape[0]):
        halo_ref[p] = halo[p * slots : (p + 1) * slots].astype(BF)
    hub = jnp.dot(hubs_ref[...].astype(BF), grad_agg, preferred_element_type=F32)
    hub_local = hub_ref.shape[1]
    for g in range(hub_ref.shape[0]):
        hub_ref[g] = hub[g * hub_local : (g + 1) * hub_local].astype(BF)
    own = lax.dot_general(pre_ref[...], ws_ref[...], CONTRACT_COLS, preferred_element_type=F32)
    own_ref[...] = own + jnp.dot(own_counts_ref[...].astype(BF), grad_agg, preferred_element_type=F32)


def total(in_ref, first, last):
    acc = in_ref[0].astype(F32)[first:last]
    for i in range(1, in_ref.shape[0]):
        acc = acc + in_ref[i].astype(F32)[first:last]
    return acc


def second_kernel(got_ref, halo_ref, send_ref):
    part = total(got_ref, 0, got_ref.shape[1])
    for p in range(halo_ref.shape[0]):
        send_ref[p] = jnp.concatenate([halo_ref[p].astype(F32), part], axis=0).astype(BF)


def third_kernel(got_ref, hub_ref, send_ref):
    n_grp, hub_local = hub_ref.shape[:2]
    part_rows = send_ref.shape[1] - hub_local
    slots = got_ref.shape[1] - part_rows
    part = total(got_ref, slots, slots + part_rows)
    for g in range(n_grp):
        send_ref[g] = jnp.concatenate([hub_ref[g].astype(F32), part], axis=0).astype(BF)


def return_kernel(own_ref, slot_ref, got_ref, out_ref):
    peers = got_ref.shape[0]
    slots = slot_ref.shape[1] // peers
    back = jnp.concatenate([got_ref[p].astype(F32)[:slots] for p in range(peers)], axis=0).astype(BF)
    out_ref[...] = own_ref[...] + jnp.dot(slot_ref[...], back, preferred_element_type=F32)


def last_kernel(in_ref, hubs_ref, self_ref, neigh_ref):
    width = self_ref.shape[0]
    n_grp, send_rows = in_ref.shape[:2]
    hub_local = hubs_ref.shape[0]
    part_rows = send_rows - hub_local
    hubs_ref[...] = total(in_ref, 0, hub_local)
    per = width // part_rows
    for i, ref in enumerate((self_ref, neigh_ref)):
        for j in range(2):
            for n in range(per):
                block = in_ref[(2 * i + j) * per + n].astype(F32)[hub_local:]
                ref[n * part_rows : (n + 1) * part_rows, j * 128 : (j + 1) * 128] = block


def exchange(value, axis):
    return lax.all_to_all(value, axis, split_axis=0, concat_axis=0, tiled=True)


def on_device(features, hub_features, nbr_ids, hub_ids, halo_rows, w_self, w_neigh, grad_hidden):
    rows, width = features.shape
    hidden_width = w_self.shape[1]
    n_dom = lax.axis_size("dom")
    n_grp = lax.axis_size("grp")
    slots = halo_rows.shape[1]
    hub_local = hub_features.shape[0]
    hubs = hub_local * n_grp
    halo = n_dom * slots

    part_rows = 4 * width // n_grp

    (hub_copies,) = staged(copies_kernel, [shape((n_grp, hub_local, width), BF)], [hub_features], 0)
    all_hubs = exchange(hub_copies, "grp").reshape(hubs, width)
    (outgoing,) = staged(
        pack_kernel, [shape((n_dom, slots, width), BF)], [halo_rows, features], 2 * halo * rows * width
    )
    own_counts, halo_counts, hub_counts, slot_pick = staged(
        count_kernel,
        [shape((rows, rows), I8), shape((halo, rows), I8), shape((hubs, rows), I8), shape((rows, halo), BF)],
        [nbr_ids.T, hub_ids.T, halo_rows],
        10**9,
    )
    outgoing, all_hubs, own_counts, halo_counts, hub_counts, slot_pick = lax.optimization_barrier(
        (outgoing, all_hubs, own_counts, halo_counts, hub_counts, slot_pick)
    )
    incoming = exchange(outgoing, "dom").reshape(halo, width)
    (agg_part,) = staged(
        hub_kernel,
        [shape((width, rows), F32)],
        [hub_counts, all_hubs, features, own_counts],
        2 * rows * width * (hubs + rows),
    )
    hidden, grad_pre, grad_agg, send = staged(
        forward_kernel,
        [
            shape((rows, hidden_width), BF),
            shape((rows, hidden_width), BF),
            shape((rows, width), BF),
            shape((n_grp, part_rows, width), BF),
        ],
        [incoming, features, halo_counts, agg_part, w_self, w_neigh, grad_hidden],
        2 * rows * width * (halo + 4 * hidden_width),
    )
    got = exchange(send, "grp")
    halo_part, own, hub_part = call(
        backward_kernel,
        [
            shape((n_dom, slots, width), BF),
            shape((rows, width), F32),
            shape((n_grp, hub_local, width), BF),
        ],
        [own_counts, halo_counts, hub_counts, grad_pre, grad_agg, w_self],
        2 * rows * width * (rows + halo + hubs + hidden_width),
    )
    (send,) = call(second_kernel, [shape((n_dom, slots + part_rows, width), BF)], [got, halo_part], 0)
    back = exchange(send, "dom")
    (send,) = call(
        third_kernel, [shape((n_grp, hub_local + part_rows, width), BF)], [back, hub_part], 0
    )
    whole = exchange(send, "grp")
    (grad_features,) = call(
        return_kernel, [shape((rows, width), F32)], [own, slot_pick, back], 2 * rows * halo * width
    )
    grad_hubs, grad_w_self, grad_w_neigh = call(
        last_kernel,
        [shape((hub_local, width), F32), *[shape((width, hidden_width), F32)] * 2],
        [whole],
        0,
    )
    return (hidden, grad_features, grad_hubs, grad_w_self, grad_w_neigh)


def solution(mesh):
    both = P(("dom", "grp"), None)
    return jax.shard_map(
        on_device,
        mesh=mesh,
        in_specs=(both, both, both, both, both, P(), P(), both),
        out_specs=(both, both, both, P(), P()),
        check_vma=False,
    )
```
